32 devices in a mesh: groups: 2 (over x), enc: 16 (over z, y, core).
Axes of the slice: x: 2, y: 2, z: 4, core: 2. Of those that a mesh axis runs over, the one named last changes fastest.
Arguments:
- decoder_states: bfloat16 [128, 64, 768], P(('groups', 'enc')), parts along dimension 0, may hold values from -40 to 40
- cotangent: bfloat16 [128, 64, 768], P(('groups', 'enc')), parts along dimension 0, may hold values from -6 to 6
- encoded: bfloat16 [1024, 16, 768], P(('groups', 'enc')), parts along dimension 0, may hold values from -80 to 80
- valid_len: int32 [1024], P(('groups', 'enc')), parts along dimension 0, may hold values from 1 to 16
- retrieved: int32 [128, 16], P(('groups', 'enc')), parts along dimension 0, may hold values from 0 to 511, as said below
- w_query: bfloat16 [768, 768], replicated, may hold values from -0.21875 to 0.21875
- w_key: bfloat16 [768, 768], replicated, may hold values from -0.21875 to 0.21875
- w_value: bfloat16 [768, 768], replicated, may hold values from -0.21875 to 0.21875
- w_output: bfloat16 [768, 768], replicated, may hold values from -0.21875 to 0.21875
Outputs:
- attended: bfloat16 [128, 64, 768], P(('groups', 'enc')), parts along dimension 0
- d_decoder: bfloat16 [128, 64, 768], P(('groups', 'enc')), parts along dimension 0
- d_encoded: bfloat16 [1024, 16, 768], P(('groups', 'enc')), parts along dimension 0
- grad_query: float32 [1536, 768], P(('groups', 'enc')), parts along dimension 0
- grad_key: float32 [1536, 768], P(('groups', 'enc')), parts along dimension 0
- grad_value: float32 [1536, 768], P(('groups', 'enc')), parts along dimension 0
- grad_output: float32 [1536, 768], P(('groups', 'enc')), parts along dimension 0
The draws below stay inside these ranges and needn't reach their ends.
There are 2 independent parts, one for each index of `groups`. The reference program is written for one: setup_inputs(seed, part) draws one part's arguments, and reference() takes and returns one part's arrays. A program takes and returns all parts, laid end to end along the dimension named above; an argument that names none is the same for every part. Nothing has to cross between parts.
Inputs may be any that keep to these rules, and one draw needn't show every extreme that they name: `retrieved`: passage p lives on device p // 32 of enc. Among the 64 ids of the questions of one device, no device owns more than 8; in each group one device owns exactly 8 of the ids of every device's questions. Ids may repeat within a question.
All inputs are finite; a program needn't handle non-finite values.
Results may differ from the reference program's by a relative error of at most 0.012.
The reference program's roundings to bfloat16 on the way (of `queries`, `probs_b`, `context`, `value_grad` and `score_grad`) count: a program that leaves them out, or rounds other values in their place, can miss the bound.
Values may be sent and summed in bfloat16 or wider, within the bound.
A program may use at most 128 MiB of HBM per device.

```python
import math
import jax
import jax.numpy as jnp
from jax import lax

D = 768
HEADS = 12
DEC = 64
K_RET = 16
L = 16
Q_DEV = 4
P_DEV = 32
QUESTIONS = 64
PASSAGES = 512
CAP = 8
N_ENC = 16


def owner_block(block_key, hot_owner):
    first_key, second_key, third_key = jax.random.split(block_key, 3)
    slot_count = Q_DEV * K_RET
    tickets = jnp.arange(N_ENC * CAP, dtype=jnp.int32) // CAP
    shuffled = tickets[jax.random.permutation(first_key, N_ENC * CAP)]
    front_key = jnp.where(shuffled == hot_owner, 0, 1).astype(jnp.int32)
    ordered = shuffled[jnp.argsort(front_key, stable=True)]
    chosen = jax.random.permutation(second_key, ordered[:slot_count])
    local_ids = jax.random.randint(third_key, (slot_count,), 0, P_DEV, dtype=jnp.int32)
    return (chosen * P_DEV + local_ids).astype(jnp.int32).reshape(Q_DEV, K_RET)


def draw_retrieved(key, part):
    key = jax.random.fold_in(key, 11)
    hot_owner = jax.random.randint(jax.random.fold_in(key, 1), (), 0, N_ENC, dtype=jnp.int32)
    block_keys = jax.random.split(jax.random.fold_in(key, 2), N_ENC)
    blocks = jax.vmap(owner_block, in_axes=(0, None))(block_keys, hot_owner)
    return blocks.reshape(N_ENC * Q_DEV, K_RET)


def draw_decoder_states(key, part):
    key = jax.random.fold_in(key, 21)
    base = jax.random.truncated_normal(key, -5.0, 5.0, (QUESTIONS, DEC, D), jnp.float32)
    return base.astype(jnp.bfloat16)


def draw_encoded(key, part):
    key = jax.random.fold_in(key, 31)
    base = jax.random.truncated_normal(key, -5.0, 5.0, (PASSAGES, L, D), jnp.float32)
    return base.astype(jnp.bfloat16)


def set_ends(values, stream_key, least, largest):
    index_at = [jax.random.randint(jax.random.fold_in(stream_key, axis), (), 0, length) for axis, length in enumerate(values.shape)]
    longest = values.shape.index(max(values.shape))
    neighbour = index_at[:longest] + [(index_at[longest] + 1) % values.shape[longest]] + index_at[longest + 1:]
    return values.at[tuple(index_at)].set(least).at[tuple(neighbour)].set(largest)


def steps_of(key, shape, pieces, least, high):
    loudness = 1.0
    for dim, parts in pieces:
        steps = jax.random.uniform(jax.random.fold_in(jax.random.fold_in(key, 6), dim), (parts,), jnp.float32, least / len(pieces), high / len(pieces))
        loudness = loudness * jnp.repeat(jnp.exp(steps), shape[dim] // parts).reshape((-1,) + (1,) * (len(shape) - 1 - dim))
    return loudness


def scatter_about(key, extent, deviation, most, cuts=(), held_as=jnp.bfloat16):
    factor_of = steps_of(key, extent, cuts, -0.22, 0.18) if cuts else 1.0
    entries = jax.random.normal(key, extent, jnp.float32) * deviation * factor_of
    return jnp.minimum(jnp.maximum(entries, -most), most).astype(held_as)


def setup_inputs(seed: int = 0, part: int = 0) -> dict:
    streams_of = jax.random.split(jax.random.key(seed), 10)
    part_splits = jax.random.split(jax.random.fold_in(streams_of[9], part), 10)
    return {
        "decoder_states": draw_decoder_states(jax.random.fold_in(jax.random.fold_in(streams_of[9], part), 71), part),
        "cotangent": scatter_about(part_splits[1], (QUESTIONS, DEC, D), 1.0, 6.0, ((0, 16),)),
        "encoded": draw_encoded(jax.random.fold_in(jax.random.fold_in(streams_of[9], part), 71), part),
        "valid_len": set_ends(jax.random.randint(part_splits[3], (PASSAGES,), 1, L + 1), jax.random.fold_in(part_splits[3], 1), 1, L).astype(jnp.int32),
        "retrieved": draw_retrieved(jax.random.fold_in(jax.random.fold_in(streams_of[9], part), 71), part),
        "w_query": scatter_about(streams_of[5], (D, D), D ** -0.5, 0.21875),
        "w_key": scatter_about(streams_of[6], (D, D), D ** -0.5, 0.21875),
        "w_value": scatter_about(streams_of[7], (D, D), D ** -0.5, 0.21875),
        "w_output": scatter_about(streams_of[8], (D, D), D ** -0.5, 0.21875),
    }


def attend_core(queries, key_rows, value_rows, key_live, context_grad, score_scale):
    q32 = queries.astype(jnp.float32)
    k32 = key_rows.astype(jnp.float32)
    v32 = value_rows.astype(jnp.float32)
    g32 = context_grad.astype(jnp.float32)
    scores = jnp.einsum('qthd,qshd->qhts', q32, k32) * score_scale
    scores = jnp.where(key_live[:, None, None, :], scores, -1e+30)
    top = lax.optimization_barrier(jnp.max(scores, axis=-1, keepdims=True))
    expo = jnp.exp(scores - top)
    probs = expo / lax.optimization_barrier(jnp.sum(expo, axis=-1, keepdims=True))
    probs_b = probs.astype(jnp.bfloat16)
    pb32 = probs_b.astype(jnp.float32)
    context = jnp.einsum('qhts,qshd->qthd', pb32, v32).astype(jnp.bfloat16)
    prob_grad = jnp.einsum('qthd,qshd->qhts', g32, v32)
    value_grad = jnp.einsum('qhts,qthd->qshd', pb32, g32).astype(jnp.bfloat16)
    inner = lax.optimization_barrier(jnp.sum(probs * prob_grad, axis=-1, keepdims=True))
    score_grad = (probs * (prob_grad - inner) * score_scale).astype(jnp.bfloat16)
    sg32 = score_grad.astype(jnp.float32)
    query_grad = jnp.einsum('qhts,qshd->qthd', sg32, k32).astype(jnp.bfloat16)
    key_grad = jnp.einsum('qhts,qthd->qshd', sg32, q32).astype(jnp.bfloat16)
    return (context, query_grad, key_grad, value_grad)

def reference(decoder_states, cotangent, encoded, valid_len, retrieved, w_query, w_key, w_value, w_output):
    head_dim = D // HEADS
    score_scale = 1.0 / math.sqrt(head_dim)
    enc_flat = encoded.reshape(PASSAGES * L, D)
    key_table = jnp.dot(enc_flat, w_key, preferred_element_type=jnp.float32).astype(jnp.bfloat16).reshape(PASSAGES, L, D)
    value_table = jnp.dot(enc_flat, w_value, preferred_element_type=jnp.float32).astype(jnp.bfloat16).reshape(PASSAGES, L, D)
    dec_flat = decoder_states.reshape(QUESTIONS * DEC, D)
    cot_flat = cotangent.reshape(QUESTIONS * DEC, D)
    queries = jnp.dot(dec_flat, w_query, preferred_element_type=jnp.float32).astype(jnp.bfloat16).reshape(QUESTIONS, DEC, HEADS, head_dim)
    context_grad = jnp.dot(cot_flat, w_output.T, preferred_element_type=jnp.float32).astype(jnp.bfloat16).reshape(QUESTIONS, DEC, HEADS, head_dim)
    token_pos = jnp.arange(L, dtype=jnp.int32)

    def step(carry, xs):
        acc_key, acc_value = carry
        one_query, one_grad, id_list = xs
        key_rows = key_table[id_list].reshape(1, K_RET * L, HEADS, head_dim)
        value_rows = value_table[id_list].reshape(1, K_RET * L, HEADS, head_dim)
        key_live = (token_pos[None, :] < valid_len[id_list][:, None]).reshape(1, K_RET * L)
        context, query_grad, key_grad, value_grad = attend_core(one_query[None], key_rows, value_rows, key_live, one_grad[None], score_scale)
        acc_key = acc_key.at[id_list].add(key_grad.reshape(K_RET, L, D).astype(jnp.float32))
        acc_value = acc_value.at[id_list].add(value_grad.reshape(K_RET, L, D).astype(jnp.float32))
        return ((acc_key, acc_value), (context[0], query_grad[0]))
    zeros = jnp.zeros((PASSAGES, L, D), jnp.float32)
    (acc_key, acc_value), (contexts, query_grads) = lax.scan(step, (zeros, zeros), (queries, context_grad, retrieved))
    ctx_flat = contexts.reshape(QUESTIONS * DEC, D)
    qg_flat = query_grads.reshape(QUESTIONS * DEC, D)
    attended = jnp.dot(ctx_flat, w_output, preferred_element_type=jnp.float32).astype(jnp.bfloat16).reshape(QUESTIONS, DEC, D)
    grad_output = jnp.dot(ctx_flat.T, cot_flat, preferred_element_type=jnp.float32)
    d_decoder = jnp.dot(qg_flat, w_query.T, preferred_element_type=jnp.float32).astype(jnp.bfloat16).reshape(QUESTIONS, DEC, D)
    grad_query = jnp.dot(dec_flat.T, qg_flat, preferred_element_type=jnp.float32)
    key_sum = acc_key.reshape(PASSAGES * L, D)
    value_sum = acc_value.reshape(PASSAGES * L, D)
    highest = lax.Precision.HIGHEST
    d_encoded = (jnp.dot(key_sum, w_key.astype(jnp.float32).T, precision=highest) + jnp.dot(value_sum, w_value.astype(jnp.float32).T, precision=highest)).astype(jnp.bfloat16).reshape(PASSAGES, L, D)
    enc32 = enc_flat.astype(jnp.float32)
    grad_key = jnp.dot(enc32.T, key_sum, precision=highest)
    grad_value = jnp.dot(enc32.T, value_sum, precision=highest)
    return (attended, d_decoder, d_encoded, grad_query, grad_key, grad_value, grad_output)
```

```python
import functools
import math

import jax
import jax.numpy as jnp
from jax import lax
from jax.experimental import pallas as pl
from jax.experimental.pallas import tpu as pltpu
from jax.sharding import PartitionSpec as P

HEADS = 12
MESH = pl.DeviceIdType.MESH
BF = jnp.bfloat16
F32 = jnp.float32


def place(me):
    return me // 4, (me // 2) % 2, me % 2


def index_of(z, y, c):
    return z * 4 + y * 2 + c


def greet_all(n, me):
    barrier = pltpu.get_barrier_semaphore()
    for k in range(1, n):
        pl.semaphore_signal(
            barrier, inc=1, device_id={"enc": lax.rem(me + k, n)}, device_id_type=MESH
        )
    pl.semaphore_wait(barrier, n - 1)


def gather_kernel(
    n, cut, enc_ref, info_ref, table_ref, infos_ref, send_sem, recv_sem, info_send, info_recv, own_sem
):
    depth = n // 4
    me = lax.axis_index("enc")
    z, y, c = place(me)
    rows = enc_ref.shape[0]
    spans = (pl.ds(0, cut), pl.ds(cut, rows - cut))
    greet_all(n, me)

    owns = [pltpu.make_async_copy(enc_ref, table_ref.at[me], own_sem.at[0])]
    owns.append(pltpu.make_async_copy(info_ref, infos_ref.at[me], own_sem.at[1]))
    sends = []

    def send(cond, src, origin, half, kind, target):
        copy = pltpu.make_async_remote_copy(
            src_ref=src,
            dst_ref=table_ref.at[origin, spans[half]],
            send_sem=send_sem.at[kind, half, origin],
            recv_sem=recv_sem.at[half, origin],
            device_id={"enc": target},
            device_id_type=MESH,
        )
        sends.append((cond, copy))
        if cond is None:
            copy.start()
        else:
            pl.when(cond)(copy.start)

    def arrive(cond, origin, half):
        copy = pltpu.make_async_remote_copy(
            src_ref=table_ref.at[origin, spans[half]],
            dst_ref=table_ref.at[origin, spans[half]],
            send_sem=send_sem.at[0, half, origin],
            recv_sem=recv_sem.at[half, origin],
            device_id={"enc": me},
            device_id_type=MESH,
        )
        if cond is None:
            copy.wait_recv()
        else:
            pl.when(cond)(copy.wait_recv)

    up_ok, down_ok = z < depth - 1, z > 0
    up = index_of(jnp.minimum(z + 1, depth - 1), y, c)
    down = index_of(jnp.maximum(z - 1, 0), y, c)
    across = index_of(z, 1 - y, c)
    sibling = index_of(z, y, 1 - c)

    own = [enc_ref.at[span] for span in spans]
    send(None, own[1], me, 1, 2, across)
    send(up_ok, own[0], me, 0, 0, up)
    send(down_ok, own[0], me, 0, 1, down)
    send(None, own[0], me, 0, 2, across)
    send(up_ok, own[1], me, 1, 0, up)
    send(down_ok, own[1], me, 1, 1, down)
    for half in range(2):
        send(None, own[half], me, half, 3, sibling)
    info_copies = []
    for k in range(1, n):
        copy = pltpu.make_async_remote_copy(
            src_ref=info_ref,
            dst_ref=infos_ref.at[me],
            send_sem=info_send.at[k],
            recv_sem=info_recv.at[me],
            device_id={"enc": lax.rem(me + k, n)},
            device_id_type=MESH,
        )
        copy.start()
        info_copies.append(copy)
    for copy in owns:
        copy.start()

    def passed(cond, origin, half, go_up, go_down, go_across):
        arrive(cond, origin, half)
        block = table_ref.at[origin, spans[half]]
        both = lambda a: a if cond is None else jnp.logical_and(cond, a)
        if go_up:
            send(both(up_ok), block, origin, half, 0, up)
        if go_down:
            send(both(down_ok), block, origin, half, 1, down)
        if go_across:
            send(cond, block, origin, half, 2, across)
        send(cond, block, origin, half, 3, sibling)

    passed(None, across, 1, True, True, False)
    for d in range(1, depth):
        for sign in (1, -1):
            zo = z - sign * d
            cond = jnp.logical_and(zo >= 0, zo < depth)
            zc = jnp.clip(zo, 0, depth - 1)
            passed(cond, index_of(zc, y, c), 0, sign > 0, sign < 0, True)
            passed(cond, index_of(zc, y, c), 1, sign > 0, sign < 0, False)
            passed(cond, index_of(zc, 1 - y, c), 1, sign > 0, sign < 0, False)
        if d == 1:
            passed(None, across, 0, False, False, False)
        for sign in (1, -1):
            zo = z - sign * d
            cond = jnp.logical_and(zo >= 0, zo < depth)
            zc = jnp.clip(zo, 0, depth - 1)
            passed(cond, index_of(zc, 1 - y, c), 0, False, False, False)
    for zo in range(depth):
        for yo in range(2):
            for half in range(2):
                arrive(None, index_of(zo, yo, 1 - c), half)
    for cond, copy in sends:
        if cond is None:
            copy.wait_send()
        else:
            pl.when(cond)(copy.wait_send)
    for k in range(1, n):
        info_copies[k - 1].wait_send()
        source = lax.rem(me + n - k, n)
        pltpu.make_async_remote_copy(
            src_ref=info_ref,
            dst_ref=infos_ref.at[source],
            send_sem=info_send.at[k],
            recv_sem=info_recv.at[source],
            device_id={"enc": source},
            device_id_type=MESH,
        ).wait_recv()
    for copy in owns:
        copy.wait()


def gather_all(encoded_flat, info, n):
    rows, width = encoded_flat.shape
    cut = rows * 13 // 16 // 16 * 16
    hbm = pl.BlockSpec(memory_space=pl.ANY)
    return pl.pallas_call(
        functools.partial(gather_kernel, n, cut),
        out_shape=(
            jax.ShapeDtypeStruct((n, rows, width), BF),
            jax.ShapeDtypeStruct((n,) + info.shape, jnp.int32),
        ),
        in_specs=[hbm, hbm],
        out_specs=(hbm, hbm),
        scratch_shapes=[
            pltpu.SemaphoreType.DMA((4, 2, n)),
            pltpu.SemaphoreType.DMA((2, n)),
            pltpu.SemaphoreType.DMA((n,)),
            pltpu.SemaphoreType.DMA((n,)),
            pltpu.SemaphoreType.DMA((2,)),
        ],
        compiler_params=pltpu.CompilerParams(collective_id=0, has_side_effects=True),
        name="gather_passages",
    )(encoded_flat, info)


def return_kernel(
    n, slots_ref, g_ref, got_ref, gout_ref, r1, s1, r2, s2, r3, sem1, sem2, send3, recv3, send_a, recv_a, own_sem
):
    depth = n // 4
    me = lax.axis_index("enc")
    z, y, c = place(me)
    sibling = index_of(z, y, 1 - c)
    across = index_of(z, 1 - y, c)
    greet_all(n, me)

    def remote(src, dst, ssem, rsem, target):
        return pltpu.make_async_remote_copy(
            src_ref=src, dst_ref=dst, send_sem=ssem, recv_sem=rsem,
            device_id={"enc": target}, device_id_type=MESH,
        )

    first = remote(g_ref.at[1 - c], r1, sem1.at[0], sem1.at[1], sibling)
    first.start()
    slot_copies = []
    for k in range(1, n):
        target = lax.rem(me + k, n)
        copy = remote(slots_ref.at[target], got_ref.at[me], send_a.at[k], recv_a.at[me], target)
        copy.start()
        slot_copies.append(copy)
    own = pltpu.make_async_copy(slots_ref.at[me], got_ref.at[me], own_sem)
    own.start()
    first.wait()

    def add1(i, carry):
        for yy in range(2):
            s1[yy, i] = (g_ref[c, yy, i].astype(F32) + r1[yy, i].astype(F32)).astype(BF)
        return carry

    lax.fori_loop(0, depth, add1, 0)
    second = remote(s1.at[1 - y], r2, sem2.at[0], sem2.at[1], across)
    second.start()
    second.wait()

    def add2(i, carry):
        s2[i] = (s1[y, i].astype(F32) + r2[i].astype(F32)).astype(BF)
        return carry

    lax.fori_loop(0, depth, add2, 0)
    thirds = []
    for k in range(1, depth):
        zt = lax.rem(z + k, depth)
        copy = remote(s2.at[zt], r3.at[z], send3.at[k], recv3.at[z], index_of(zt, y, c))
        copy.start()
        thirds.append(copy)
    for k in range(1, depth):
        thirds[k - 1].wait_send()
        zs = lax.rem(z + depth - k, depth)
        remote(s2.at[zs], r3.at[zs], send3.at[k], recv3.at[zs], index_of(zs, y, c)).wait_recv()
    gout_ref[...] = s2[z].astype(F32)
    for k in range(1, depth):
        gout_ref[...] += r3[lax.rem(z + k, depth)].astype(F32)
    for k in range(1, n):
        slot_copies[k - 1].wait_send()
        source = lax.rem(me + n - k, n)
        remote(slots_ref.at[source], got_ref.at[source], send_a.at[k], recv_a.at[source], source).wait_recv()
    own.wait()


def return_all(slots, grads, n):
    depth = n // 4
    high, width = grads.shape[-2:]
    hbm = pl.BlockSpec(memory_space=pl.ANY)
    vmem = pl.BlockSpec(memory_space=pltpu.VMEM)
    return pl.pallas_call(
        functools.partial(return_kernel, n),
        out_shape=(
            jax.ShapeDtypeStruct(slots.shape, BF),
            jax.ShapeDtypeStruct((high, width), F32),
        ),
        in_specs=[hbm, vmem],
        out_specs=(hbm, vmem),
        scratch_shapes=[
            pltpu.VMEM((2, depth, high, width), BF),
            pltpu.VMEM((2, depth, high, width), BF),
            pltpu.VMEM((depth, high, width), BF),
            pltpu.VMEM((depth, high, width), BF),
            pltpu.VMEM((depth, high, width), BF),
            pltpu.SemaphoreType.DMA((2,)),
            pltpu.SemaphoreType.DMA((2,)),
            pltpu.SemaphoreType.DMA((depth,)),
            pltpu.SemaphoreType.DMA((depth,)),
            pltpu.SemaphoreType.DMA((n,)),
            pltpu.SemaphoreType.DMA((n,)),
            pltpu.SemaphoreType.DMA(()),
        ],
        compiler_params=pltpu.CompilerParams(
            collective_id=1, has_side_effects=True, vmem_limit_bytes=48 * 2**20
        ),
        name="return_gradients",
    )(slots, grads)


def attend_core(queries, key_rows, value_rows, key_live, context_grad, score_scale):
    scores = (
        jnp.einsum("qthd,qshd->qhts", queries, key_rows, preferred_element_type=F32) * score_scale
    )
    scores = jnp.where(key_live[:, None, None, :], scores, -1e30)
    top = jnp.max(scores, axis=-1, keepdims=True)
    expo = jnp.exp(scores - top)
    probs = expo / jnp.sum(expo, axis=-1, keepdims=True)
    probs_b = probs.astype(BF)
    context = jnp.einsum("qhts,qshd->qthd", probs_b, value_rows, preferred_element_type=F32).astype(BF)
    prob_grad = jnp.einsum("qthd,qshd->qhts", context_grad, value_rows, preferred_element_type=F32)
    value_grad = jnp.einsum("qhts,qthd->qshd", probs_b, context_grad, preferred_element_type=F32).astype(BF)
    inner = jnp.sum(probs * prob_grad, axis=-1, keepdims=True)
    score_grad = (probs * (prob_grad - inner) * score_scale).astype(BF)
    query_grad = jnp.einsum("qhts,qshd->qthd", score_grad, key_rows, preferred_element_type=F32).astype(BF)
    key_grad = jnp.einsum("qhts,qthd->qshd", score_grad, queries, preferred_element_type=F32).astype(BF)
    return (context, query_grad, key_grad, value_grad)


def body(
    decoder_states, cotangent, encoded, valid_len, retrieved, w_query, w_key, w_value, w_output
):
    n = lax.axis_size("enc")
    me = lax.axis_index("enc")
    questions_here, dec_len, width = decoder_states.shape
    passages_here, passage_len, _ = encoded.shape
    per_question = retrieved.shape[1]
    slot_count = questions_here * per_question
    cap = max(2, 2 * slot_count // n)
    head_dim = width // HEADS
    scale = 1.0 / math.sqrt(head_dim)
    ids = retrieved.reshape(slot_count)
    info = jnp.zeros((8, 128), jnp.int32).at[0, :slot_count].set(ids)
    info = info.at[1, :passages_here].set(valid_len)
    table, infos = gather_all(encoded.reshape(passages_here * passage_len, width), info, n)

    owner = ids // passages_here
    order = jnp.arange(slot_count, dtype=jnp.int32)
    before = order[None, :] < order[:, None]
    rank = jnp.sum((owner[:, None] == owner[None, :]) & before, axis=1).astype(jnp.int32)
    position = owner * cap + rank
    all_ids = infos[:, 0, :slot_count]
    lens = infos[:, 1, :passages_here].reshape(n * passages_here)

    slot_rows = table.reshape(n * passages_here, passage_len, width)[ids].reshape(
        slot_count * passage_len, width
    )
    slot_len = lens[ids]
    token_pos = jnp.arange(passage_len, dtype=jnp.int32)
    key_live = (token_pos[None, :] < slot_len[:, None]).reshape(
        questions_here, per_question * passage_len
    )
    dec_flat = decoder_states.reshape(questions_here * dec_len, width)
    cot_flat = cotangent.reshape(questions_here * dec_len, width)
    head_shape = (questions_here, dec_len, HEADS, head_dim)
    kv_shape = (questions_here, per_question * passage_len, HEADS, head_dim)
    dot = functools.partial(jnp.dot, preferred_element_type=F32)
    queries = dot(dec_flat, w_query).astype(BF).reshape(head_shape)
    context_grad = dot(cot_flat, w_output.T).astype(BF).reshape(head_shape)
    keys = dot(slot_rows, w_key).astype(BF)
    values = dot(slot_rows, w_value).astype(BF)
    context, query_grad, key_grad, value_grad = attend_core(
        queries, keys.reshape(kv_shape), values.reshape(kv_shape), key_live, context_grad, scale
    )
    ctx = context.reshape(questions_here * dec_len, width)
    qg = query_grad.reshape(questions_here * dec_len, width)
    kg = key_grad.reshape(slot_count * passage_len, width)
    vg = value_grad.reshape(slot_count * passage_len, width)
    attended = dot(ctx, w_output).astype(BF)
    d_decoder = dot(qg, w_query.T).astype(BF)
    share = (dot(kg, w_key.T) + dot(vg, w_value.T)).astype(BF)
    slots = (
        jnp.zeros((n * cap, passage_len, width), BF)
        .at[position]
        .set(share.reshape(slot_count, passage_len, width))
        .reshape(n, cap * passage_len, width)
    )
    parts = [dot(dec_flat.T, qg), dot(slot_rows.T, kg), dot(slot_rows.T, vg), dot(ctx.T, cot_flat)]
    rows = width // n
    grads = jnp.stack([part.astype(BF) for part in parts])
    grads = grads.reshape(4, n // 4, 2, 2, rows, width).transpose(3, 2, 1, 0, 4, 5)
    grads = grads.reshape(2, 2, n // 4, 4 * rows, width)
    got, summed = return_all(slots, grads, n)

    ask_owner = all_ids // passages_here
    before_b = before.astype(F32)
    mine = (ask_owner == me).astype(F32)
    ranks = jnp.einsum("si,ji->sj", mine, before_b)
    wanted_hot = (
        (all_ids[:, :, None] == me * passages_here + jnp.arange(passages_here))[:, :, None, :]
        & (ranks[:, :, None, None] == jnp.arange(cap, dtype=F32)[None, None, :, None])
    )
    select = jnp.any(wanted_hot, axis=1).astype(BF).reshape(n * cap, passages_here)
    d_encoded = lax.dot_general(
        select,
        got.reshape(n * cap, passage_len * width),
        (((0,), (0,)), ((), ())),
        preferred_element_type=F32,
    ).astype(BF)
    return (
        attended.reshape(decoder_states.shape),
        d_decoder.reshape(decoder_states.shape),
        d_encoded.reshape(encoded.shape),
        summed[0 * rows : 1 * rows],
        summed[1 * rows : 2 * rows],
        summed[2 * rows : 3 * rows],
        summed[3 * rows : 4 * rows],
    )


def solution(mesh):
    both = ("groups", "enc")
    in_specs = (
        P(both, None, None),
        P(both, None, None),
        P(both, None, None),
        P(both),
        P(both, None),
        P(),
        P(),
        P(),
        P(),
    )
    out_specs = (
        P(both, None, None),
        P(both, None, None),
        P(both, None, None),
        P(both, None),
        P(both, None),
        P(both, None),
        P(both, None),
    )
    return jax.shard_map(body, mesh=mesh, in_specs=in_specs, out_specs=out_specs, check_vma=False)
```

```python
import functools
import math

import jax
import jax.numpy as jnp
from jax import lax
from jax.experimental import pallas as pl
from jax.experimental.pallas import tpu as pltpu
from jax.sharding import PartitionSpec as P

HEADS = 12
MESH = pl.DeviceIdType.MESH
BF = jnp.bfloat16
F32 = jnp.float32


def place(me):
    return me // 4, (me // 2) % 2, me % 2


def index_of(z, y, c):
    return z * 4 + y * 2 + c


def greet_all(n, me):
    barrier = pltpu.get_barrier_semaphore()
    for k in range(1, n):
        pl.semaphore_signal(
            barrier, inc=1, device_id={"enc": lax.rem(me + k, n)}, device_id_type=MESH
        )
    pl.semaphore_wait(barrier, n - 1)


def gather_kernel(
    n, cut, enc_ref, info_ref, table_ref, infos_ref, send_sem, recv_sem, info_send, info_recv, own_sem
):
    depth = n // 4
    me = lax.axis_index("enc")
    z, y, c = place(me)
    rows = enc_ref.shape[0]
    spans = (pl.ds(0, cut), pl.ds(cut, rows - cut))
    greet_all(n, me)

    owns = [pltpu.make_async_copy(enc_ref, table_ref.at[me], own_sem.at[0])]
    owns.append(pltpu.make_async_copy(info_ref, infos_ref.at[me], own_sem.at[1]))
    sends = []

    def send(cond, src, origin, half, kind, target):
        copy = pltpu.make_async_remote_copy(
            src_ref=src,
            dst_ref=table_ref.at[origin, spans[half]],
            send_sem=send_sem.at[kind, half, origin],
            recv_sem=recv_sem.at[half, origin],
            device_id={"enc": target},
            device_id_type=MESH,
        )
        sends.append((cond, copy))
        if cond is None:
            copy.start()
        else:
            pl.when(cond)(copy.start)

    def arrive(cond, origin, half):
        copy = pltpu.make_async_remote_copy(
            src_ref=table_ref.at[origin, spans[half]],
            dst_ref=table_ref.at[origin, spans[half]],
            send_sem=send_sem.at[0, half, origin],
            recv_sem=recv_sem.at[half, origin],
            device_id={"enc": me},
            device_id_type=MESH,
        )
        if cond is None:
            copy.wait_recv()
        else:
            pl.when(cond)(copy.wait_recv)

    up_ok, down_ok = z < depth - 1, z > 0
    up = index_of(jnp.minimum(z + 1, depth - 1), y, c)
    down = index_of(jnp.maximum(z - 1, 0), y, c)
    across = index_of(z, 1 - y, c)
    sibling = index_of(z, y, 1 - c)

    own = [enc_ref.at[span] for span in spans]
    send(None, own[1], me, 1, 2, across)
    send(up_ok, own[0], me, 0, 0, up)
    send(down_ok, own[0], me, 0, 1, down)
    send(None, own[0], me, 0, 2, across)
    send(up_ok, own[1], me, 1, 0, up)
    send(down_ok, own[1], me, 1, 1, down)
    for half in range(2):
        send(None, own[half], me, half, 3, sibling)
    info_copies = []
    for k in range(1, n):
        copy = pltpu.make_async_remote_copy(
            src_ref=info_ref,
            dst_ref=infos_ref.at[me],
            send_sem=info_send.at[k],
            recv_sem=info_recv.at[me],
            device_id={"enc": lax.rem(me + k, n)},
            device_id_type=MESH,
        )
        copy.start()
        info_copies.append(copy)
    for copy in owns:
        copy.start()

    def passed(cond, origin, half, go_up, go_down, go_across):
        arrive(cond, origin, half)
        block = table_ref.at[origin, spans[half]]
        both = lambda a: a if cond is None else jnp.logical_and(cond, a)
        if go_up:
            send(both(up_ok), block, origin, half, 0, up)
        if go_down:
            send(both(down_ok), block, origin, half, 1, down)
        if go_across:
            send(cond, block, origin, half, 2, across)
        send(cond, block, origin, half, 3, sibling)

    passed(None, across, 1, True, True, False)
    for d in range(1, depth):
        for sign in (1, -1):
            zo = z - sign * d
            cond = jnp.logical_and(zo >= 0, zo < depth)
            zc = jnp.clip(zo, 0, depth - 1)
            passed(cond, index_of(zc, y, c), 0, sign > 0, sign < 0, True)
            passed(cond, index_of(zc, y, c), 1, sign > 0, sign < 0, False)
            passed(cond, index_of(zc, 1 - y, c), 1, sign > 0, sign < 0, False)
        if d == 1:
            passed(None, across, 0, False, False, False)
        for sign in (1, -1):
            zo = z - sign * d
            cond = jnp.logical_and(zo >= 0, zo < depth)
            zc = jnp.clip(zo, 0, depth - 1)
            passed(cond, index_of(zc, 1 - y, c), 0, False, False, False)
    for zo in range(depth):
        for yo in range(2):
            for half in range(2):
                arrive(None, index_of(zo, yo, 1 - c), half)
    for cond, copy in sends:
        if cond is None:
            copy.wait_send()
        else:
            pl.when(cond)(copy.wait_send)
    for k in range(1, n):
        info_copies[k - 1].wait_send()
        source = lax.rem(me + n - k, n)
        pltpu.make_async_remote_copy(
            src_ref=info_ref,
            dst_ref=infos_ref.at[source],
            send_sem=info_send.at[k],
            recv_sem=info_recv.at[source],
            device_id={"enc": source},
            device_id_type=MESH,
        ).wait_recv()
    for copy in owns:
        copy.wait()


def gather_all(encoded_flat, info, n):
    rows, width = encoded_flat.shape
    cut = rows * 13 // 16 // 16 * 16
    hbm = pl.BlockSpec(memory_space=pl.ANY)
    return pl.pallas_call(
        functools.partial(gather_kernel, n, cut),
        out_shape=(
            jax.ShapeDtypeStruct((n, rows, width), BF),
            jax.ShapeDtypeStruct((n,) + info.shape, jnp.int32),
        ),
        in_specs=[hbm, hbm],
        out_specs=(hbm, hbm),
        scratch_shapes=[
            pltpu.SemaphoreType.DMA((4, 2, n)),
            pltpu.SemaphoreType.DMA((2, n)),
            pltpu.SemaphoreType.DMA((n,)),
            pltpu.SemaphoreType.DMA((n,)),
            pltpu.SemaphoreType.DMA((2,)),
        ],
        compiler_params=pltpu.CompilerParams(collective_id=0, has_side_effects=True),
        name="gather_passages",
    )(encoded_flat, info)


def return_kernel(
    n, slots_ref, g_ref, got_ref, gout_ref, r1, s1, r2, s2, r3, sem1, sem2, send3, recv3, send_a, recv_a, own_sem
):
    depth = n // 4
    me = lax.axis_index("enc")
    z, y, c = place(me)
    sibling = index_of(z, y, 1 - c)
    across = index_of(z, 1 - y, c)
    greet_all(n, me)

    def remote(src, dst, ssem, rsem, target):
        return pltpu.make_async_remote_copy(
            src_ref=src, dst_ref=dst, send_sem=ssem, recv_sem=rsem,
            device_id={"enc": target}, device_id_type=MESH,
        )

    first = remote(g_ref.at[1 - c], r1, sem1.at[0], sem1.at[1], sibling)
    first.start()
    slot_copies = []
    for k in range(1, n):
        target = lax.rem(me + k, n)
        copy = remote(slots_ref.at[target], got_ref.at[me], send_a.at[k], recv_a.at[me], target)
        copy.start()
        slot_copies.append(copy)
    own = pltpu.make_async_copy(slots_ref.at[me], got_ref.at[me], own_sem)
    own.start()
    first.wait()

    def add1(i, carry):
        for yy in range(2):
            s1[yy, i] = (g_ref[c, yy, i].astype(F32) + r1[yy, i].astype(F32)).astype(BF)
        return carry

    lax.fori_loop(0, depth, add1, 0)
    second = remote(s1.at[1 - y], r2, sem2.at[0], sem2.at[1], across)
    second.start()
    second.wait()

    def add2(i, carry):
        s2[i] = (s1[y, i].astype(F32) + r2[i].astype(F32)).astype(BF)
        return carry

    lax.fori_loop(0, depth, add2, 0)
    thirds = []
    for k in range(1, depth):
        zt = lax.rem(z + k, depth)
        copy = remote(s2.at[zt], r3.at[z], send3.at[k], recv3.at[z], index_of(zt, y, c))
        copy.start()
        thirds.append(copy)
    for k in range(1, depth):
        thirds[k - 1].wait_send()
        zs = lax.rem(z + depth - k, depth)
        remote(s2.at[zs], r3.at[zs], send3.at[k], recv3.at[zs], index_of(zs, y, c)).wait_recv()
    gout_ref[...] = s2[z].astype(F32)
    for k in range(1, depth):
        gout_ref[...] += r3[lax.rem(z + k, depth)].astype(F32)
    for k in range(1, n):
        slot_copies[k - 1].wait_send()
        source = lax.rem(me + n - k, n)
        remote(slots_ref.at[source], got_ref.at[source], send_a.at[k], recv_a.at[source], source).wait_recv()
    own.wait()


def return_all(slots, grads, n):
    depth = n // 4
    block = grads.shape[-3:]
    hbm = pl.BlockSpec(memory_space=pl.ANY)
    vmem = pl.BlockSpec(memory_space=pltpu.VMEM)
    return pl.pallas_call(
        functools.partial(return_kernel, n),
        out_shape=(
            jax.ShapeDtypeStruct(slots.shape, BF),
            jax.ShapeDtypeStruct(block, F32),
        ),
        in_specs=[hbm, vmem],
        out_specs=(hbm, vmem),
        scratch_shapes=[
            pltpu.VMEM((2, depth) + block, BF),
            pltpu.VMEM((2, depth) + block, BF),
            pltpu.VMEM((depth,) + block, BF),
            pltpu.VMEM((depth,) + block, BF),
            pltpu.VMEM((depth,) + block, BF),
            pltpu.SemaphoreType.DMA((2,)),
            pltpu.SemaphoreType.DMA((2,)),
            pltpu.SemaphoreType.DMA((depth,)),
            pltpu.SemaphoreType.DMA((depth,)),
            pltpu.SemaphoreType.DMA((n,)),
            pltpu.SemaphoreType.DMA((n,)),
            pltpu.SemaphoreType.DMA(()),
        ],
        compiler_params=pltpu.CompilerParams(
            collective_id=1, has_side_effects=True, vmem_limit_bytes=48 * 2**20
        ),
        name="return_gradients",
    )(slots, grads)


def attend_kernel(
    n, cap, per_owner, dims, ids_ref, infos_ref, dec_ref, cot_ref, table_ref, wq_ref, wk_ref, wv_ref, wo_ref,
    att_ref, ddec_ref, slots_ref, g_ref,
    rows, rows_t, keys, values, kg, vg, queries, cgrad, ctx, qg, flip, bias, counts, where_to, sems,
):
    questions, tokens, slots_per, length = dims
    slot_count = questions * slots_per
    span = slots_per * length
    width = dec_ref.shape[1]
    scale = 1.0 / math.sqrt(width // HEADS)
    high = width // n
    tile = 256

    def nn(a, b):
        return lax.dot_general(a, b, (((1,), (0,)), ((), ())), preferred_element_type=F32)

    def nt(a, b):
        return lax.dot_general(a, b, (((1,), (1,)), ((), ())), preferred_element_type=F32)

    def tn(a, b):
        return lax.dot_general(a, b, (((0,), (0,)), ((), ())), preferred_element_type=F32)

    def fetch(j):
        return pltpu.make_async_copy(
            table_ref.at[ids_ref[j]], rows.at[pl.ds(j * length, length)], sems.at[j]
        )

    def clear(i, carry):
        counts[i] = 0
        return carry

    lax.fori_loop(0, n, clear, 0)
    token_at = lax.broadcasted_iota(jnp.int32, (length, 128), 0)

    def begin(j, carry):
        fetch(j).start()
        passage = ids_ref[j]
        owner = passage // per_owner
        where_to[j] = owner * cap + counts[owner]
        counts[owner] = counts[owner] + 1
        live = infos_ref[owner, 1, passage - owner * per_owner]
        bias[pl.ds(pl.multiple_of(j * length, length), length), :] = jnp.where(token_at < live, 0.0, -1e30)
        return carry

    lax.fori_loop(0, slot_count, begin, 0)

    def wipe(i, carry):
        slots_ref[i] = jnp.zeros((length, width), BF)
        return carry

    lax.fori_loop(0, n * cap, wipe, 0)
    queries[...] = nn(dec_ref[...], wq_ref[...]).astype(BF)
    cgrad[...] = nt(cot_ref[...], wo_ref[...]).astype(BF)

    def finish(j, carry):
        fetch(j).wait()
        return carry

    lax.fori_loop(0, slot_count, finish, 0)

    def project(i, carry):
        at = pl.ds(pl.multiple_of(i * span, span), span)
        block = rows[at, :]
        keys[at, :] = nn(block, wk_ref[...]).astype(BF)
        values[at, :] = nn(block, wv_ref[...]).astype(BF)
        rows_t[:, at] = block.T
        return carry

    lax.fori_loop(0, questions, project, 0)
    low = lax.broadcasted_iota(jnp.int32, (tokens, 128), 1) < 64

    def attend(q, carry):
        kat = pl.ds(pl.multiple_of(q * span, span), span)
        tat = pl.ds(pl.multiple_of(q * tokens, tokens), tokens)
        dead = bias[kat, :]
        for pair in range(width // 128):
            cols = pl.ds(pair * 128, 128)
            qp, cp = queries[tat, cols], cgrad[tat, cols]
            zero = jnp.zeros_like(qp)
            q2 = jnp.concatenate([jnp.where(low, qp, zero), jnp.where(low, zero, qp)], axis=0)
            c2 = jnp.concatenate([jnp.where(low, cp, zero), jnp.where(low, zero, cp)], axis=0)
            kp, vp = keys[kat, cols], values[kat, cols]
            scores = nt(kp, q2) * scale + dead
            top = jnp.max(scores, axis=0, keepdims=True)
            expo = jnp.exp(scores - top)
            probs = expo / jnp.sum(expo, axis=0, keepdims=True)
            probs_b = probs.astype(BF)
            both = tn(probs_b, vp)
            ctx[tat, cols] = jnp.where(low, both[:tokens], both[tokens:]).astype(BF)
            vg[kat, cols] = nn(probs_b, c2).astype(BF)
            pgrad = nt(vp, c2)
            inner = jnp.sum(probs * pgrad, axis=0, keepdims=True)
            sgrad = (probs * (pgrad - inner) * scale).astype(BF)
            both_q = tn(sgrad, kp)
            qg[tat, cols] = jnp.where(low, both_q[:tokens], both_q[tokens:]).astype(BF)
            kg[kat, cols] = nn(sgrad, q2).astype(BF)
        return carry

    lax.fori_loop(0, questions, attend, 0)
    att_ref[...] = nn(ctx[...], wo_ref[...]).astype(BF)
    ddec_ref[...] = nt(qg[...], wq_ref[...]).astype(BF)

    def back(i, carry):
        at = pl.ds(pl.multiple_of(i * span, span), span)
        share = (nt(kg[at, :], wk_ref[...]) + nt(vg[at, :], wv_ref[...])).astype(BF)
        for j in range(slots_per):
            slots_ref[where_to[i * slots_per + j]] = share[j * length : (j + 1) * length]
        return carry

    lax.fori_loop(0, questions, back, 0)

    def spread(which, left, right):
        def one(i, carry):
            cols = pl.ds(pl.multiple_of(i * tile, tile), tile)
            part = nn(left[...], right[:, cols])
            for e in range(n):
                z, y, c = place(e)
                g_ref[c, y, z, which, :, cols] = part[e * high : (e + 1) * high].astype(BF)
            return carry

        lax.fori_loop(0, width // tile, one, 0)

    spread(1, rows_t, kg)
    spread(2, rows_t, vg)
    flip[...] = dec_ref[...].T
    spread(0, flip, qg)
    flip[...] = ctx[...].T
    spread(3, flip, cot_ref)


def attend_all(ids, infos, dec, cot, table, weights, n, cap, dims):
    questions, tokens, slots_per, length = dims
    width = dec.shape[1]
    slot_rows = questions * slots_per * length
    smem = pl.BlockSpec(memory_space=pltpu.SMEM)
    vmem = pl.BlockSpec(memory_space=pltpu.VMEM)
    hbm = pl.BlockSpec(memory_space=pl.ANY)
    shape = jax.ShapeDtypeStruct
    return pl.pallas_call(
        functools.partial(attend_kernel, n, cap, table.shape[0] // n, dims),
        out_shape=(
            shape(dec.shape, BF),
            shape(dec.shape, BF),
            shape((n * cap, length, width), BF),
            shape((2, 2, n // 4, 4, width // n, width), BF),
        ),
        in_specs=[smem, smem, vmem, vmem, hbm, vmem, vmem, vmem, vmem],
        out_specs=(vmem,) * 4,
        scratch_shapes=[
            pltpu.VMEM((slot_rows, width), BF),
            pltpu.VMEM((width, slot_rows), BF),
            pltpu.VMEM((slot_rows, width), BF),
            pltpu.VMEM((slot_rows, width), BF),
            pltpu.VMEM((slot_rows, width), BF),
            pltpu.VMEM((slot_rows, width), BF),
            pltpu.VMEM(dec.shape, BF),
            pltpu.VMEM(dec.shape, BF),
            pltpu.VMEM(dec.shape, BF),
            pltpu.VMEM(dec.shape, BF),
            pltpu.VMEM((width, dec.shape[0]), BF),
            pltpu.VMEM((slot_rows, 128), F32),
            pltpu.SMEM((n,), jnp.int32),
            pltpu.SMEM((questions * slots_per,), jnp.int32),
            pltpu.SemaphoreType.DMA((questions * slots_per,)),
        ],
        compiler_params=pltpu.CompilerParams(vmem_limit_bytes=56 * 2**20),
        name="attend",
    )(ids, infos, dec, cot, table, *weights)


def body(
    decoder_states, cotangent, encoded, valid_len, retrieved, w_query, w_key, w_value, w_output
):
    n = lax.axis_size("enc")
    me = lax.axis_index("enc")
    questions_here, dec_len, width = decoder_states.shape
    passages_here, passage_len, _ = encoded.shape
    per_question = retrieved.shape[1]
    slot_count = questions_here * per_question
    cap = max(2, 2 * slot_count // n)
    ids = retrieved.reshape(slot_count)
    info = jnp.zeros((8, 128), jnp.int32).at[0, :slot_count].set(ids)
    info = info.at[1, :passages_here].set(valid_len)
    table, infos = gather_all(encoded.reshape(passages_here * passage_len, width), info, n)

    all_ids = infos[:, 0, :slot_count]
    attended, d_decoder, slots, grads = attend_all(
        ids,
        infos,
        decoder_states.reshape(questions_here * dec_len, width),
        cotangent.reshape(questions_here * dec_len, width),
        table.reshape(n * passages_here, passage_len, width),
        (w_query, w_key, w_value, w_output),
        n,
        cap,
        (questions_here, dec_len, per_question, passage_len),
    )
    got, summed = return_all(slots.reshape(n, cap * passage_len, width), grads, n)

    ask_owner = all_ids // passages_here
    order = jnp.arange(slot_count, dtype=jnp.int32)
    before = (order[:, None] < order[None, :]).astype(F32)
    mine = ask_owner == me
    ranks = jnp.dot(mine.astype(F32), before)
    hit = mine[:, None, :] & (ranks[:, None, :] == jnp.arange(cap, dtype=F32)[None, :, None])
    local = all_ids - me * passages_here + 1
    wanted = jnp.sum(jnp.where(hit, local[:, None, :], 0), axis=2) - 1
    token_pos = jnp.arange(passage_len, dtype=jnp.int32)
    sent_row = (wanted[:, :, None] * passage_len + token_pos).reshape(n * cap * passage_len)
    sent_row = jnp.where(sent_row < 0, -1, sent_row)
    own_row = jnp.arange(passages_here * passage_len, dtype=jnp.int32)
    select = (own_row[:, None] == sent_row[None, :]).astype(BF)
    d_encoded = jnp.dot(
        select, got.reshape(n * cap * passage_len, width), preferred_element_type=F32
    ).astype(BF)
    return (
        attended.reshape(decoder_states.shape),
        d_decoder.reshape(decoder_states.shape),
        d_encoded.reshape(encoded.shape),
        summed[0],
        summed[1],
        summed[2],
        summed[3],
    )


def solution(mesh):
    both = ("groups", "enc")
    in_specs = (
        P(both, None, None),
        P(both, None, None),
        P(both, None, None),
        P(both),
        P(both, None),
        P(),
        P(),
        P(),
        P(),
    )
    out_specs = (
        P(both, None, None),
        P(both, None, None),
        P(both, None, None),
        P(both, None),
        P(both, None),
        P(both, None),
        P(both, None),
    )
    return jax.shard_map(body, mesh=mesh, in_specs=in_specs, out_specs=out_specs, check_vma=False)
```

```python
import functools
import math

import jax
import jax.numpy as jnp
from jax import lax
from jax.experimental import pallas as pl
from jax.experimental.pallas import tpu as pltpu
from jax.sharding import PartitionSpec as P

HEADS = 12
MESH = pl.DeviceIdType.MESH
BF = jnp.bfloat16
F32 = jnp.float32


def place(me):
    return me // 4, (me // 2) % 2, me % 2


def index_of(z, y, c):
    return z * 4 + y * 2 + c


def greet_all(n, me):
    barrier = pltpu.get_barrier_semaphore()
    for k in range(1, n):
        pl.semaphore_signal(
            barrier, inc=1, device_id={"enc": lax.rem(me + k, n)}, device_id_type=MESH
        )
    pl.semaphore_wait(barrier, n - 1)


def gather_kernel(
    n, cuts, enc_ref, ids_ref, len_ref, table_ref, infos_ref,
    info_ref, send_sem, recv_sem, info_send, info_recv, own_sem,
):
    depth = n // 4
    me = lax.axis_index("enc")
    z, y, c = place(me)
    spans = [pl.ds(a, b - a) for a, b in zip(cuts[:-1], cuts[1:])]
    last = len(spans) - 1
    info_ref[...] = jnp.zeros_like(info_ref)
    info_ref[0 : ids_ref.shape[0], 0 : ids_ref.shape[1]] = ids_ref[...]
    info_ref[ids_ref.shape[0] : ids_ref.shape[0] + 1, 0 : len_ref.shape[1]] = len_ref[...]
    greet_all(n, me)

    owns = [pltpu.make_async_copy(enc_ref, table_ref.at[me], own_sem.at[0])]
    owns.append(pltpu.make_async_copy(info_ref, infos_ref.at[me], own_sem.at[1]))
    sends = []

    def send(cond, src, origin, part, kind, target):
        copy = pltpu.make_async_remote_copy(
            src_ref=src,
            dst_ref=table_ref.at[origin, spans[part]],
            send_sem=send_sem.at[kind, part, origin],
            recv_sem=recv_sem.at[part, origin],
            device_id={"enc": target},
            device_id_type=MESH,
        )
        sends.append((cond, copy))
        if cond is None:
            copy.start()
        else:
            pl.when(cond)(copy.start)

    def arrive(cond, origin, part):
        copy = pltpu.make_async_remote_copy(
            src_ref=table_ref.at[origin, spans[part]],
            dst_ref=table_ref.at[origin, spans[part]],
            send_sem=send_sem.at[0, part, origin],
            recv_sem=recv_sem.at[part, origin],
            device_id={"enc": me},
            device_id_type=MESH,
        )
        if cond is None:
            copy.wait_recv()
        else:
            pl.when(cond)(copy.wait_recv)

    up_ok, down_ok = z < depth - 1, z > 0
    up = index_of(jnp.minimum(z + 1, depth - 1), y, c)
    down = index_of(jnp.maximum(z - 1, 0), y, c)
    across = index_of(z, 1 - y, c)
    sibling = index_of(z, y, 1 - c)

    own = [enc_ref.at[span] for span in spans]
    for part in range(last):
        send(up_ok, own[part], me, part, 0, up)
        send(down_ok, own[part], me, part, 1, down)
        send(None, own[part], me, part, 2, across)
    send(None, own[last], me, last, 2, across)
    info_copies = []
    for k in range(1, n):
        copy = pltpu.make_async_remote_copy(
            src_ref=info_ref,
            dst_ref=infos_ref.at[me],
            send_sem=info_send.at[k],
            recv_sem=info_recv.at[me],
            device_id={"enc": lax.rem(me + k, n)},
            device_id_type=MESH,
        )
        copy.start()
        info_copies.append(copy)
    for part in range(last + 1):
        send(None, own[part], me, part, 3, sibling)
    for copy in owns:
        copy.start()

    def passed(cond, origin, part, go_up, go_down, go_across):
        arrive(cond, origin, part)
        block = table_ref.at[origin, spans[part]]
        both = lambda a: a if cond is None else jnp.logical_and(cond, a)
        if go_up:
            send(both(up_ok), block, origin, part, 0, up)
        if go_down:
            send(both(down_ok), block, origin, part, 1, down)
        if go_across:
            send(cond, block, origin, part, 2, across)
        send(cond, block, origin, part, 3, sibling)

    def along(d, sign):
        zo = z - sign * d
        return jnp.logical_and(zo >= 0, zo < depth), jnp.clip(zo, 0, depth - 1)

    def late(d):
        if d == 0:
            send(up_ok, own[last], me, last, 0, up)
            send(down_ok, own[last], me, last, 1, down)
            passed(None, across, last, True, True, False)
            return
        for sign in (1, -1):
            cond, zc = along(d, sign)
            for row in (y, 1 - y):
                passed(cond, index_of(zc, row, c), last, sign > 0, sign < 0, False)

    def crossed(d):
        for part in range(last):
            if d == 0:
                passed(None, across, part, False, False, False)
                continue
            for sign in (1, -1):
                cond, zc = along(d, sign)
                passed(cond, index_of(zc, 1 - y, c), part, False, False, False)

    for d in range(1, depth):
        for part in range(last):
            for sign in (1, -1):
                cond, zc = along(d, sign)
                passed(cond, index_of(zc, y, c), part, sign > 0, sign < 0, True)
        late(d - 1)
        crossed(d - 1)
    late(depth - 1)
    crossed(depth - 1)
    for zo in range(depth):
        for yo in range(2):
            for part in range(last + 1):
                arrive(None, index_of(zo, yo, 1 - c), part)
    for cond, copy in sends:
        if cond is None:
            copy.wait_send()
        else:
            pl.when(cond)(copy.wait_send)
    for k in range(1, n):
        info_copies[k - 1].wait_send()
        source = lax.rem(me + n - k, n)
        pltpu.make_async_remote_copy(
            src_ref=info_ref,
            dst_ref=infos_ref.at[source],
            send_sem=info_send.at[k],
            recv_sem=info_recv.at[source],
            device_id={"enc": source},
            device_id_type=MESH,
        ).wait_recv()
    for copy in owns:
        copy.wait()


def gather_all(encoded_flat, retrieved, valid_len, n):
    rows, width = encoded_flat.shape
    cut = rows * 13 // 16 // 32 * 32
    cuts = (0, cut // 2, cut, rows)
    parts = len(cuts) - 1
    hbm = pl.BlockSpec(memory_space=pl.ANY)
    vmem = pl.BlockSpec(memory_space=pltpu.VMEM)
    return pl.pallas_call(
        functools.partial(gather_kernel, n, cuts),
        out_shape=(
            jax.ShapeDtypeStruct((n, rows, width), BF),
            jax.ShapeDtypeStruct((n, 8, 128), jnp.int32),
        ),
        in_specs=[hbm, vmem, vmem],
        out_specs=(hbm, hbm),
        scratch_shapes=[
            pltpu.VMEM((8, 128), jnp.int32),
            pltpu.SemaphoreType.DMA((4, parts, n)),
            pltpu.SemaphoreType.DMA((parts, n)),
            pltpu.SemaphoreType.DMA((n,)),
            pltpu.SemaphoreType.DMA((n,)),
            pltpu.SemaphoreType.DMA((2,)),
        ],
        compiler_params=pltpu.CompilerParams(collective_id=0, has_side_effects=True),
        name="gather_passages",
    )(encoded_flat, retrieved, valid_len)


def return_kernel(
    n, slots_ref, g_ref, got_ref, gout_ref, r1, s1, r2, s2, s3, r3, sem1, sem2, send3, recv3, send_a, recv_a, own_sem
):
    depth = n // 4
    me = lax.axis_index("enc")
    z, y, c = place(me)
    sibling = index_of(z, y, 1 - c)
    across = index_of(z, 1 - y, c)
    greet_all(n, me)

    def remote(src, dst, ssem, rsem, target):
        return pltpu.make_async_remote_copy(
            src_ref=src, dst_ref=dst, send_sem=ssem, recv_sem=rsem,
            device_id={"enc": target}, device_id_type=MESH,
        )

    first = remote(g_ref.at[1 - c], r1, sem1.at[0], sem1.at[1], sibling)
    first.start()
    slot_copies = []
    for k in range(1, n):
        target = lax.rem(me + k, n)
        copy = remote(slots_ref.at[target], got_ref.at[me], send_a.at[k], recv_a.at[me], target)
        copy.start()
        slot_copies.append(copy)
    own = pltpu.make_async_copy(slots_ref.at[me], got_ref.at[me], own_sem)
    own.start()
    first.wait()

    def add1(i, carry):
        for yy in range(2):
            s1[yy, i] = (g_ref[c, yy, i].astype(F32) + r1[yy, i].astype(F32)).astype(BF)
        return carry

    lax.fori_loop(0, depth, add1, 0)
    second = remote(s1.at[1 - y], r2, sem2.at[0], sem2.at[1], across)
    second.start()
    second.wait()

    def add2(i, carry):
        s2[i] = (s1[y, i].astype(F32) + r2[i].astype(F32)).astype(BF)
        return carry

    lax.fori_loop(0, depth, add2, 0)
    for hop in range(depth - 1, 0, -1):
        for way, sign in ((0, 1), (1, -1)):
            t = z + sign * hop
            inside = jnp.logical_and(t >= 0, t < depth)
            has_back = jnp.logical_and(z - sign >= 0, z - sign < depth)
            tc = jnp.clip(t, 0, depth - 1)
            ahead = index_of(jnp.clip(z + sign, 0, depth - 1), y, c)
            behind = jnp.logical_and(inside, has_back)

            @pl.when(jnp.logical_and(inside, jnp.logical_not(has_back)))
            def _(way=way, tc=tc):
                s3[way, tc] = s2[tc]

            @pl.when(behind)
            def _(way=way, tc=tc):
                remote(s3.at[way, tc], r3.at[way, tc], send3.at[way, tc], recv3.at[way, tc], me).wait_recv()
                s3[way, tc] = (s2[tc].astype(F32) + r3[way, tc].astype(F32)).astype(BF)

            @pl.when(inside)
            def _(way=way, tc=tc, ahead=ahead):
                remote(s3.at[way, tc], r3.at[way, tc], send3.at[way, tc], recv3.at[way, tc], ahead).start()

    gout_ref[...] = s2[z].astype(F32)
    for way, sign in ((0, 1), (1, -1)):

        @pl.when(jnp.logical_and(z - sign >= 0, z - sign < depth))
        def _(way=way):
            remote(s3.at[way, z], r3.at[way, z], send3.at[way, z], recv3.at[way, z], me).wait_recv()
            gout_ref[...] += r3[way, z].astype(F32)

    for hop in range(1, depth):
        for way, sign in ((0, 1), (1, -1)):
            t = z + sign * hop
            tc = jnp.clip(t, 0, depth - 1)

            @pl.when(jnp.logical_and(t >= 0, t < depth))
            def _(way=way, tc=tc):
                remote(s3.at[way, tc], r3.at[way, tc], send3.at[way, tc], recv3.at[way, tc], me).wait_send()

    for k in range(1, n):
        slot_copies[k - 1].wait_send()
        source = lax.rem(me + n - k, n)
        remote(slots_ref.at[source], got_ref.at[source], send_a.at[k], recv_a.at[source], source).wait_recv()
    own.wait()


def return_all(slots, grads, n):
    depth = n // 4
    block = grads.shape[-3:]
    hbm = pl.BlockSpec(memory_space=pl.ANY)
    vmem = pl.BlockSpec(memory_space=pltpu.VMEM)
    return pl.pallas_call(
        functools.partial(return_kernel, n),
        out_shape=(
            jax.ShapeDtypeStruct(slots.shape, BF),
            jax.ShapeDtypeStruct(block, F32),
        ),
        in_specs=[hbm, vmem],
        out_specs=(hbm, vmem),
        scratch_shapes=[
            pltpu.VMEM((2, depth) + block, BF),
            pltpu.VMEM((2, depth) + block, BF),
            pltpu.VMEM((depth,) + block, BF),
            pltpu.VMEM((depth,) + block, BF),
            pltpu.VMEM((2, depth) + block, BF),
            pltpu.VMEM((2, depth) + block, BF),
            pltpu.SemaphoreType.DMA((2,)),
            pltpu.SemaphoreType.DMA((2,)),
            pltpu.SemaphoreType.DMA((2, depth)),
            pltpu.SemaphoreType.DMA((2, depth)),
            pltpu.SemaphoreType.DMA((n,)),
            pltpu.SemaphoreType.DMA((n,)),
            pltpu.SemaphoreType.DMA(()),
        ],
        compiler_params=pltpu.CompilerParams(
            collective_id=1, has_side_effects=True, vmem_limit_bytes=48 * 2**20
        ),
        name="return_gradients",
    )(slots, grads)


def attend_kernel(
    n, cap, per_owner, dims, ids_ref, infos_ref, dec_ref, cot_ref, table_ref, wq_ref, wk_ref, wv_ref, wo_ref,
    att_ref, ddec_ref, slots_ref, g_ref,
    rows, rows_t, keys, values, kg, vg, queries, cgrad, ctx, qg, flip, bias, counts, where_to, sems,
):
    questions, tokens, slots_per, length = dims
    slot_count = questions * slots_per
    span = slots_per * length
    width = dec_ref.shape[1]
    scale = 1.0 / math.sqrt(width // HEADS)
    high = width // n
    tile = 256

    def nn(a, b):
        return lax.dot_general(a, b, (((1,), (0,)), ((), ())), preferred_element_type=F32)

    def nt(a, b):
        return lax.dot_general(a, b, (((1,), (1,)), ((), ())), preferred_element_type=F32)

    def tn(a, b):
        return lax.dot_general(a, b, (((0,), (0,)), ((), ())), preferred_element_type=F32)

    def fetch(j):
        return pltpu.make_async_copy(
            table_ref.at[ids_ref[j // slots_per, j % slots_per]], rows.at[pl.ds(j * length, length)], sems.at[j]
        )

    def clear(i, carry):
        counts[i] = 0
        return carry

    lax.fori_loop(0, n, clear, 0)
    token_at = lax.broadcasted_iota(jnp.int32, (length, 128), 0)

    def begin(j, carry):
        fetch(j).start()
        passage = ids_ref[j // slots_per, j % slots_per]
        owner = passage // per_owner
        where_to[j] = owner * cap + counts[owner]
        counts[owner] = counts[owner] + 1
        live = infos_ref[owner, questions, passage - owner * per_owner]
        bias[pl.ds(pl.multiple_of(j * length, length), length), :] = jnp.where(token_at < live, 0.0, -1e30)
        return carry

    lax.fori_loop(0, slot_count, begin, 0)

    def wipe(i, carry):
        slots_ref[i] = jnp.zeros((length, width), BF)
        return carry

    lax.fori_loop(0, n * cap, wipe, 0)
    queries[...] = nn(dec_ref[...], wq_ref[...]).astype(BF)
    cgrad[...] = nt(cot_ref[...], wo_ref[...]).astype(BF)

    def finish(j, carry):
        fetch(j).wait()
        return carry

    lax.fori_loop(0, slot_count, finish, 0)

    def project(i, carry):
        at = pl.ds(pl.multiple_of(i * span, span), span)
        block = rows[at, :]
        keys[at, :] = nn(block, wk_ref[...]).astype(BF)
        values[at, :] = nn(block, wv_ref[...]).astype(BF)
        rows_t[:, at] = block.T
        return carry

    lax.fori_loop(0, questions, project, 0)
    low = lax.broadcasted_iota(jnp.int32, (tokens, 128), 1) < 64

    def attend(q, carry):
        kat = pl.ds(pl.multiple_of(q * span, span), span)
        tat = pl.ds(pl.multiple_of(q * tokens, tokens), tokens)
        dead = bias[kat, :]
        for pair in range(width // 128):
            cols = pl.ds(pair * 128, 128)
            qp, cp = queries[tat, cols], cgrad[tat, cols]
            zero = jnp.zeros_like(qp)
            q2 = jnp.concatenate([jnp.where(low, qp, zero), jnp.where(low, zero, qp)], axis=0)
            c2 = jnp.concatenate([jnp.where(low, cp, zero), jnp.where(low, zero, cp)], axis=0)
            kp, vp = keys[kat, cols], values[kat, cols]
            scores = nt(kp, q2) * scale + dead
            top = jnp.max(scores, axis=0, keepdims=True)
            expo = jnp.exp(scores - top)
            probs = expo * (1.0 / jnp.sum(expo, axis=0, keepdims=True))
            probs_b = probs.astype(BF)
            both = tn(probs_b, vp)
            ctx[tat, cols] = jnp.where(low, both[:tokens], both[tokens:]).astype(BF)
            vg[kat, cols] = nn(probs_b, c2).astype(BF)
            pgrad = nt(vp, c2)
            inner = jnp.sum(probs * pgrad, axis=0, keepdims=True)
            sgrad = (probs * (pgrad - inner) * scale).astype(BF)
            both_q = tn(sgrad, kp)
            qg[tat, cols] = jnp.where(low, both_q[:tokens], both_q[tokens:]).astype(BF)
            kg[kat, cols] = nn(sgrad, q2).astype(BF)
        return carry

    lax.fori_loop(0, questions, attend, 0)
    att_ref[...] = nn(ctx[...], wo_ref[...]).astype(BF)
    ddec_ref[...] = nt(qg[...], wq_ref[...]).astype(BF)

    def back(i, carry):
        at = pl.ds(pl.multiple_of(i * span, span), span)
        share = (nt(kg[at, :], wk_ref[...]) + nt(vg[at, :], wv_ref[...])).astype(BF)
        for j in range(slots_per):
            slots_ref[where_to[i * slots_per + j]] = share[j * length : (j + 1) * length]
        return carry

    lax.fori_loop(0, questions, back, 0)

    def spread(which, left, right):
        def one(i, carry):
            cols = pl.ds(pl.multiple_of(i * tile, tile), tile)
            part = nn(left[...], right[:, cols])
            for e in range(n):
                z, y, c = place(e)
                g_ref[c, y, z, which, :, cols] = part[e * high : (e + 1) * high].astype(BF)
            return carry

        lax.fori_loop(0, width // tile, one, 0)

    spread(1, rows_t, kg)
    spread(2, rows_t, vg)
    flip[...] = dec_ref[...].T
    spread(0, flip, qg)
    flip[...] = ctx[...].T
    spread(3, flip, cot_ref)


def attend_all(ids, infos, dec, cot, table, weights, n, cap, dims):
    questions, tokens, slots_per, length = dims
    width = dec.shape[1]
    slot_rows = questions * slots_per * length
    smem = pl.BlockSpec(memory_space=pltpu.SMEM)
    vmem = pl.BlockSpec(memory_space=pltpu.VMEM)
    hbm = pl.BlockSpec(memory_space=pl.ANY)
    shape = jax.ShapeDtypeStruct
    return pl.pallas_call(
        functools.partial(attend_kernel, n, cap, table.shape[0] // n, dims),
        out_shape=(
            shape(dec.shape, BF),
            shape(dec.shape, BF),
            shape((n * cap, length, width), BF),
            shape((2, 2, n // 4, 4, width // n, width), BF),
        ),
        in_specs=[smem, smem, vmem, vmem, hbm, vmem, vmem, vmem, vmem],
        out_specs=(vmem,) * 4,
        scratch_shapes=[
            pltpu.VMEM((slot_rows, width), BF),
            pltpu.VMEM((width, slot_rows), BF),
            pltpu.VMEM((slot_rows, width), BF),
            pltpu.VMEM((slot_rows, width), BF),
            pltpu.VMEM((slot_rows, width), BF),
            pltpu.VMEM((slot_rows, width), BF),
            pltpu.VMEM(dec.shape, BF),
            pltpu.VMEM(dec.shape, BF),
            pltpu.VMEM(dec.shape, BF),
            pltpu.VMEM(dec.shape, BF),
            pltpu.VMEM((width, dec.shape[0]), BF),
            pltpu.VMEM((slot_rows, 128), F32),
            pltpu.SMEM((n,), jnp.int32),
            pltpu.SMEM((questions * slots_per,), jnp.int32),
            pltpu.SemaphoreType.DMA((questions * slots_per,)),
        ],
        compiler_params=pltpu.CompilerParams(vmem_limit_bytes=56 * 2**20),
        name="attend",
    )(ids, infos, dec, cot, table, *weights)


def body(
    decoder_states, cotangent, encoded, valid_len, retrieved, w_query, w_key, w_value, w_output
):
    n = lax.axis_size("enc")
    me = lax.axis_index("enc")
    questions_here, dec_len, width = decoder_states.shape
    passages_here, passage_len, _ = encoded.shape
    per_question = retrieved.shape[1]
    slot_count = questions_here * per_question
    cap = max(2, 2 * slot_count // n)
    table, infos = gather_all(
        encoded.reshape(passages_here * passage_len, width),
        retrieved,
        valid_len.reshape(1, passages_here),
        n,
    )
    all_ids = infos[:, :questions_here, :per_question].reshape(n, slot_count)
    attended, d_decoder, slots, grads = attend_all(
        retrieved,
        infos,
        decoder_states.reshape(questions_here * dec_len, width),
        cotangent.reshape(questions_here * dec_len, width),
        table.reshape(n * passages_here, passage_len, width),
        (w_query, w_key, w_value, w_output),
        n,
        cap,
        (questions_here, dec_len, per_question, passage_len),
    )
    got, summed = return_all(slots.reshape(n, cap * passage_len, width), grads, n)

    ask_owner = all_ids // passages_here
    order = jnp.arange(slot_count, dtype=jnp.int32)
    before = (order[:, None] < order[None, :]).astype(F32)
    mine = ask_owner == me
    ranks = jnp.dot(mine.astype(F32), before)
    hit = mine[:, None, :] & (ranks[:, None, :] == jnp.arange(cap, dtype=F32)[None, :, None])
    local = all_ids - me * passages_here + 1
    wanted = jnp.sum(jnp.where(hit, local[:, None, :], 0), axis=2) - 1
    token_pos = jnp.arange(passage_len, dtype=jnp.int32)
    sent_row = (wanted[:, :, None] * passage_len + token_pos).reshape(n * cap * passage_len)
    sent_row = jnp.where(sent_row < 0, -1, sent_row)
    own_row = jnp.arange(passages_here * passage_len, dtype=jnp.int32)
    select = (own_row[:, None] == sent_row[None, :]).astype(BF)
    d_encoded = jnp.dot(
        select, got.reshape(n * cap * passage_len, width), preferred_element_type=F32
    ).astype(BF)
    return (
        attended.reshape(decoder_states.shape),
        d_decoder.reshape(decoder_states.shape),
        d_encoded.reshape(encoded.shape),
        summed[0],
        summed[1],
        summed[2],
        summed[3],
    )


def solution(mesh):
    both = ("groups", "enc")
    in_specs = (
        P(both, None, None),
        P(both, None, None),
        P(both, None, None),
        P(both),
        P(both, None),
        P(),
        P(),
        P(),
        P(),
    )
    out_specs = (
        P(both, None, None),
        P(both, None, None),
        P(both, None, None),
        P(both, None),
        P(both, None),
        P(both, None),
        P(both, None),
    )
    return jax.shard_map(body, mesh=mesh, in_specs=in_specs, out_specs=out_specs, check_vma=False)
```

```python
import functools
import math

import jax
import jax.numpy as jnp
from jax import lax
from jax.experimental import pallas as pl
from jax.experimental.pallas import tpu as pltpu
from jax.sharding import PartitionSpec as P

HEADS = 12
MESH = pl.DeviceIdType.MESH
BF = jnp.bfloat16
F32 = jnp.float32


def place(me):
    return me // 4, (me // 2) % 2, me % 2


def index_of(z, y, c):
    return z * 4 + y * 2 + c


def greet_all(n, me):
    barrier = pltpu.get_barrier_semaphore()
    for k in range(1, n):
        pl.semaphore_signal(
            barrier, inc=1, device_id={"enc": lax.rem(me + k, n)}, device_id_type=MESH
        )
    pl.semaphore_wait(barrier, n - 1)


def gather_kernel(
    n, cuts, enc_ref, ids_ref, len_ref, table_ref, infos_ref,
    info_ref, send_sem, recv_sem, info_send, info_recv, own_sem,
):
    depth = n // 4
    me = lax.axis_index("enc")
    z, y, c = place(me)
    spans = [pl.ds(a, b - a) for a, b in zip(cuts[:-1], cuts[1:])]
    last = len(spans) - 1
    info_ref[...] = jnp.zeros_like(info_ref)
    info_ref[0 : ids_ref.shape[0], 0 : ids_ref.shape[1]] = ids_ref[...]
    info_ref[ids_ref.shape[0] : ids_ref.shape[0] + 1, 0 : len_ref.shape[1]] = len_ref[...]
    greet_all(n, me)

    owns = [pltpu.make_async_copy(enc_ref, table_ref.at[me], own_sem.at[0])]
    owns.append(pltpu.make_async_copy(info_ref, infos_ref.at[me], own_sem.at[1]))
    sends = []

    def send(cond, src, origin, part, kind, target):
        copy = pltpu.make_async_remote_copy(
            src_ref=src,
            dst_ref=table_ref.at[origin, spans[part]],
            send_sem=send_sem.at[kind, part, origin],
            recv_sem=recv_sem.at[part, origin],
            device_id={"enc": target},
            device_id_type=MESH,
        )
        sends.append((cond, copy))
        if cond is None:
            copy.start()
        else:
            pl.when(cond)(copy.start)

    def arrive(cond, origin, part):
        copy = pltpu.make_async_remote_copy(
            src_ref=table_ref.at[origin, spans[part]],
            dst_ref=table_ref.at[origin, spans[part]],
            send_sem=send_sem.at[0, part, origin],
            recv_sem=recv_sem.at[part, origin],
            device_id={"enc": me},
            device_id_type=MESH,
        )
        if cond is None:
            copy.wait_recv()
        else:
            pl.when(cond)(copy.wait_recv)

    up_ok, down_ok = z < depth - 1, z > 0
    up = index_of(jnp.minimum(z + 1, depth - 1), y, c)
    down = index_of(jnp.maximum(z - 1, 0), y, c)
    across = index_of(z, 1 - y, c)
    sibling = index_of(z, y, 1 - c)

    own = [enc_ref.at[span] for span in spans]
    for part in range(last):
        send(up_ok, own[part], me, part, 0, up)
        send(down_ok, own[part], me, part, 1, down)
        send(None, own[part], me, part, 2, across)
    send(None, own[last], me, last, 2, across)
    info_copies = []
    for k in range(1, n):
        copy = pltpu.make_async_remote_copy(
            src_ref=info_ref,
            dst_ref=infos_ref.at[me],
            send_sem=info_send.at[k],
            recv_sem=info_recv.at[me],
            device_id={"enc": lax.rem(me + k, n)},
            device_id_type=MESH,
        )
        copy.start()
        info_copies.append(copy)
    for part in range(last + 1):
        send(None, own[part], me, part, 3, sibling)
    for copy in owns:
        copy.start()

    def passed(cond, origin, part, go_up, go_down, go_across):
        arrive(cond, origin, part)
        block = table_ref.at[origin, spans[part]]
        both = lambda a: a if cond is None else jnp.logical_and(cond, a)
        if go_up:
            send(both(up_ok), block, origin, part, 0, up)
        if go_down:
            send(both(down_ok), block, origin, part, 1, down)
        if go_across:
            send(cond, block, origin, part, 2, across)
        send(cond, block, origin, part, 3, sibling)

    def along(d, sign):
        zo = z - sign * d
        return jnp.logical_and(zo >= 0, zo < depth), jnp.clip(zo, 0, depth - 1)

    def late(d):
        if d == 0:
            send(up_ok, own[last], me, last, 0, up)
            send(down_ok, own[last], me, last, 1, down)
            passed(None, across, last, True, True, False)
            return
        for sign in (1, -1):
            cond, zc = along(d, sign)
            for row in (y, 1 - y):
                passed(cond, index_of(zc, row, c), last, sign > 0, sign < 0, False)

    def crossed(d):
        for part in range(last):
            if d == 0:
                passed(None, across, part, False, False, False)
                continue
            for sign in (1, -1):
                cond, zc = along(d, sign)
                passed(cond, index_of(zc, 1 - y, c), part, False, False, False)

    for d in range(1, depth):
        for part in range(last):
            for sign in (1, -1):
                cond, zc = along(d, sign)
                passed(cond, index_of(zc, y, c), part, sign > 0, sign < 0, True)
        late(d - 1)
        crossed(d - 1)
    late(depth - 1)
    crossed(depth - 1)
    for zo in range(depth):
        for yo in range(2):
            for part in range(last + 1):
                arrive(None, index_of(zo, yo, 1 - c), part)
    for cond, copy in sends:
        if cond is None:
            copy.wait_send()
        else:
            pl.when(cond)(copy.wait_send)
    for k in range(1, n):
        info_copies[k - 1].wait_send()
        source = lax.rem(me + n - k, n)
        pltpu.make_async_remote_copy(
            src_ref=info_ref,
            dst_ref=infos_ref.at[source],
            send_sem=info_send.at[k],
            recv_sem=info_recv.at[source],
            device_id={"enc": source},
            device_id_type=MESH,
        ).wait_recv()
    for copy in owns:
        copy.wait()


def gather_all(encoded_flat, retrieved, valid_len, n):
    rows, width = encoded_flat.shape
    cut = rows * 13 // 16 // 32 * 32
    cuts = (0, cut // 2, cut, rows)
    parts = len(cuts) - 1
    hbm = pl.BlockSpec(memory_space=pl.ANY)
    vmem = pl.BlockSpec(memory_space=pltpu.VMEM)
    return pl.pallas_call(
        functools.partial(gather_kernel, n, cuts),
        out_shape=(
            jax.ShapeDtypeStruct((n, rows, width), BF),
            jax.ShapeDtypeStruct((n, 8, 128), jnp.int32),
        ),
        in_specs=[hbm, vmem, vmem],
        out_specs=(hbm, hbm),
        scratch_shapes=[
            pltpu.VMEM((8, 128), jnp.int32),
            pltpu.SemaphoreType.DMA((4, parts, n)),
            pltpu.SemaphoreType.DMA((parts, n)),
            pltpu.SemaphoreType.DMA((n,)),
            pltpu.SemaphoreType.DMA((n,)),
            pltpu.SemaphoreType.DMA((2,)),
        ],
        compiler_params=pltpu.CompilerParams(collective_id=0, has_side_effects=True),
        name="gather_passages",
    )(encoded_flat, retrieved, valid_len)


def return_kernel(
    n, slots_ref, g_ref, got_ref, gout_ref, r1, s1, r2, s2, s3, r3, sem1, sem2, send3, recv3, send_a, recv_a, own_sem
):
    depth = n // 4
    me = lax.axis_index("enc")
    z, y, c = place(me)
    sibling = index_of(z, y, 1 - c)
    across = index_of(z, 1 - y, c)
    greet_all(n, me)

    def remote(src, dst, ssem, rsem, target):
        return pltpu.make_async_remote_copy(
            src_ref=src, dst_ref=dst, send_sem=ssem, recv_sem=rsem,
            device_id={"enc": target}, device_id_type=MESH,
        )

    first = remote(g_ref.at[1 - c], r1, sem1.at[0], sem1.at[1], sibling)
    first.start()
    slot_copies = []

    def ship(target):
        copy = remote(slots_ref.at[target], got_ref.at[me], send_a.at[target], recv_a.at[me], target)
        copy.start()
        slot_copies.append(copy)

    shifts = sorted(range(1, depth), key=lambda k: abs(2 * k - depth))
    for k in shifts:
        for core in (c, 1 - c):
            ship(index_of(lax.rem(z + k, depth), y, core))
    ship(sibling)
    own = pltpu.make_async_copy(slots_ref.at[me], got_ref.at[me], own_sem)
    own.start()
    first.wait()

    def add1(i, carry):
        for yy in range(2):
            s1[yy, i] = (g_ref[c, yy, i].astype(F32) + r1[yy, i].astype(F32)).astype(BF)
        return carry

    lax.fori_loop(0, depth, add1, 0)
    second = remote(s1.at[1 - y], r2, sem2.at[0], sem2.at[1], across)
    second.start()
    for k in shifts + [0]:
        for core in (c, 1 - c):
            ship(index_of(lax.rem(z + k, depth), 1 - y, core))
    second.wait()

    def add2(i, carry):
        s2[i] = (s1[y, i].astype(F32) + r2[i].astype(F32)).astype(BF)
        return carry

    lax.fori_loop(0, depth, add2, 0)
    for hop in range(depth - 1, 0, -1):
        for way, sign in ((0, 1), (1, -1)):
            t = z + sign * hop
            inside = jnp.logical_and(t >= 0, t < depth)
            has_back = jnp.logical_and(z - sign >= 0, z - sign < depth)
            tc = jnp.clip(t, 0, depth - 1)
            ahead = index_of(jnp.clip(z + sign, 0, depth - 1), y, c)
            behind = jnp.logical_and(inside, has_back)

            @pl.when(jnp.logical_and(inside, jnp.logical_not(has_back)))
            def _(way=way, tc=tc):
                s3[way, tc] = s2[tc]

            @pl.when(behind)
            def _(way=way, tc=tc):
                remote(s3.at[way, tc], r3.at[way, tc], send3.at[way, tc], recv3.at[way, tc], me).wait_recv()
                s3[way, tc] = (s2[tc].astype(F32) + r3[way, tc].astype(F32)).astype(BF)

            @pl.when(inside)
            def _(way=way, tc=tc, ahead=ahead):
                remote(s3.at[way, tc], r3.at[way, tc], send3.at[way, tc], recv3.at[way, tc], ahead).start()

    gout_ref[...] = s2[z].astype(F32)
    for way, sign in ((0, 1), (1, -1)):

        @pl.when(jnp.logical_and(z - sign >= 0, z - sign < depth))
        def _(way=way):
            remote(s3.at[way, z], r3.at[way, z], send3.at[way, z], recv3.at[way, z], me).wait_recv()
            gout_ref[...] += r3[way, z].astype(F32)

    for hop in range(1, depth):
        for way, sign in ((0, 1), (1, -1)):
            t = z + sign * hop
            tc = jnp.clip(t, 0, depth - 1)

            @pl.when(jnp.logical_and(t >= 0, t < depth))
            def _(way=way, tc=tc):
                remote(s3.at[way, tc], r3.at[way, tc], send3.at[way, tc], recv3.at[way, tc], me).wait_send()

    for k in range(1, n):
        slot_copies[k - 1].wait_send()
        source = lax.rem(me + n - k, n)
        remote(slots_ref.at[source], got_ref.at[source], send_a.at[source], recv_a.at[source], source).wait_recv()
    own.wait()


def return_all(slots, grads, n):
    depth = n // 4
    block = grads.shape[-3:]
    hbm = pl.BlockSpec(memory_space=pl.ANY)
    vmem = pl.BlockSpec(memory_space=pltpu.VMEM)
    return pl.pallas_call(
        functools.partial(return_kernel, n),
        out_shape=(
            jax.ShapeDtypeStruct(slots.shape, BF),
            jax.ShapeDtypeStruct(block, F32),
        ),
        in_specs=[hbm, vmem],
        out_specs=(hbm, vmem),
        scratch_shapes=[
            pltpu.VMEM((2, depth) + block, BF),
            pltpu.VMEM((2, depth) + block, BF),
            pltpu.VMEM((depth,) + block, BF),
            pltpu.VMEM((depth,) + block, BF),
            pltpu.VMEM((2, depth) + block, BF),
            pltpu.VMEM((2, depth) + block, BF),
            pltpu.SemaphoreType.DMA((2,)),
            pltpu.SemaphoreType.DMA((2,)),
            pltpu.SemaphoreType.DMA((2, depth)),
            pltpu.SemaphoreType.DMA((2, depth)),
            pltpu.SemaphoreType.DMA((n,)),
            pltpu.SemaphoreType.DMA((n,)),
            pltpu.SemaphoreType.DMA(()),
        ],
        compiler_params=pltpu.CompilerParams(
            collective_id=1, has_side_effects=True, vmem_limit_bytes=48 * 2**20
        ),
        name="return_gradients",
    )(slots, grads)


def attend_kernel(
    n, cap, per_owner, dims, ids_ref, infos_ref, dec_ref, cot_ref, table_ref, wq_ref, wk_ref, wv_ref, wo_ref,
    att_ref, ddec_ref, slots_ref, g_ref,
    rows, rows_t, keys, values, kg, vg, queries, cgrad, ctx, qg, flip, bias, counts, where_to, sems,
):
    questions, tokens, slots_per, length = dims
    slot_count = questions * slots_per
    span = slots_per * length
    width = dec_ref.shape[1]
    scale = 1.0 / math.sqrt(width // HEADS)
    high = width // n
    tile = 256

    def nn(a, b):
        return lax.dot_general(a, b, (((1,), (0,)), ((), ())), preferred_element_type=F32)

    def nt(a, b):
        return lax.dot_general(a, b, (((1,), (1,)), ((), ())), preferred_element_type=F32)

    def tn(a, b):
        return lax.dot_general(a, b, (((0,), (0,)), ((), ())), preferred_element_type=F32)

    def fetch(j):
        return pltpu.make_async_copy(
            table_ref.at[ids_ref[j // slots_per, j % slots_per]], rows.at[pl.ds(j * length, length)], sems.at[j]
        )

    def clear(i, carry):
        counts[i] = 0
        return carry

    lax.fori_loop(0, n, clear, 0)
    token_at = lax.broadcasted_iota(jnp.int32, (length, 128), 0)

    def begin(j, carry):
        fetch(j).start()
        passage = ids_ref[j // slots_per, j % slots_per]
        owner = passage // per_owner
        where_to[j] = owner * cap + counts[owner]
        counts[owner] = counts[owner] + 1
        live = infos_ref[owner, questions, passage - owner * per_owner]
        bias[pl.ds(pl.multiple_of(j * length, length), length), :] = jnp.where(token_at < live, 0.0, -1e30)
        return carry

    lax.fori_loop(0, slot_count, begin, 0)

    def wipe(i, carry):
        slots_ref[i] = jnp.zeros((length, width), BF)
        return carry

    lax.fori_loop(0, n * cap, wipe, 0)
    queries[...] = nn(dec_ref[...], wq_ref[...]).astype(BF)
    cgrad[...] = nt(cot_ref[...], wo_ref[...]).astype(BF)

    def finish(j, carry):
        fetch(j).wait()
        return carry

    lax.fori_loop(0, slot_count, finish, 0)

    def project(i, carry):
        at = pl.ds(pl.multiple_of(i * span, span), span)
        block = rows[at, :]
        keys[at, :] = nn(block, wk_ref[...]).astype(BF)
        values[at, :] = nn(block, wv_ref[...]).astype(BF)
        rows_t[:, at] = block.T
        return carry

    lax.fori_loop(0, questions, project, 0)
    low = lax.broadcasted_iota(jnp.int32, (tokens, 128), 1) < 64

    def attend(q, carry):
        kat = pl.ds(pl.multiple_of(q * span, span), span)
        tat = pl.ds(pl.multiple_of(q * tokens, tokens), tokens)
        dead = bias[kat, :]
        for pair in range(width // 128):
            cols = pl.ds(pair * 128, 128)
            qp, cp = queries[tat, cols], cgrad[tat, cols]
            zero = jnp.zeros_like(qp)
            q2 = jnp.concatenate([jnp.where(low, qp, zero), jnp.where(low, zero, qp)], axis=0)
            c2 = jnp.concatenate([jnp.where(low, cp, zero), jnp.where(low, zero, cp)], axis=0)
            q2 = q2 * jnp.asarray(scale, BF)
            kp, vp = keys[kat, cols], values[kat, cols]
            scores = nt(kp, q2) + dead
            top = jnp.max(scores, axis=0, keepdims=True)
            expo = jnp.exp(scores - top)
            probs = expo * (1.0 / jnp.sum(expo, axis=0, keepdims=True))
            probs_b = probs.astype(BF)
            both = tn(probs_b, vp)
            ctx[tat, cols] = jnp.where(low, both[:tokens], both[tokens:]).astype(BF)
            vg[kat, cols] = nn(probs_b, c2).astype(BF)
            pgrad = nt(vp, c2)
            inner = jnp.sum(probs * pgrad, axis=0, keepdims=True)
            sgrad = (probs * (pgrad - inner)).astype(BF)
            both_q = tn(sgrad, kp) * scale
            qg[tat, cols] = jnp.where(low, both_q[:tokens], both_q[tokens:]).astype(BF)
            kg[kat, cols] = nn(sgrad, q2).astype(BF)
        return carry

    lax.fori_loop(0, questions, attend, 0)
    att_ref[...] = nn(ctx[...], wo_ref[...]).astype(BF)
    ddec_ref[...] = nt(qg[...], wq_ref[...]).astype(BF)

    def back(i, carry):
        at = pl.ds(pl.multiple_of(i * span, span), span)
        share = (nt(kg[at, :], wk_ref[...]) + nt(vg[at, :], wv_ref[...])).astype(BF)
        for j in range(slots_per):
            slots_ref[where_to[i * slots_per + j]] = share[j * length : (j + 1) * length]
        return carry

    lax.fori_loop(0, questions, back, 0)

    def spread(which, left, right):
        def one(i, carry):
            cols = pl.ds(pl.multiple_of(i * tile, tile), tile)
            part = nn(left[...], right[:, cols])
            for e in range(n):
                z, y, c = place(e)
                g_ref[c, y, z, which, :, cols] = part[e * high : (e + 1) * high].astype(BF)
            return carry

        lax.fori_loop(0, width // tile, one, 0)

    spread(1, rows_t, kg)
    spread(2, rows_t, vg)
    flip[...] = dec_ref[...].T
    spread(0, flip, qg)
    flip[...] = ctx[...].T
    spread(3, flip, cot_ref)


def attend_all(ids, infos, dec, cot, table, weights, n, cap, dims):
    questions, tokens, slots_per, length = dims
    width = dec.shape[1]
    slot_rows = questions * slots_per * length
    smem = pl.BlockSpec(memory_space=pltpu.SMEM)
    vmem = pl.BlockSpec(memory_space=pltpu.VMEM)
    hbm = pl.BlockSpec(memory_space=pl.ANY)
    shape = jax.ShapeDtypeStruct
    return pl.pallas_call(
        functools.partial(attend_kernel, n, cap, table.shape[0] // n, dims),
        out_shape=(
            shape(dec.shape, BF),
            shape(dec.shape, BF),
            shape((n * cap, length, width), BF),
            shape((2, 2, n // 4, 4, width // n, width), BF),
        ),
        in_specs=[smem, smem, vmem, vmem, hbm, vmem, vmem, vmem, vmem],
        out_specs=(vmem,) * 4,
        scratch_shapes=[
            pltpu.VMEM((slot_rows, width), BF),
            pltpu.VMEM((width, slot_rows), BF),
            pltpu.VMEM((slot_rows, width), BF),
            pltpu.VMEM((slot_rows, width), BF),
            pltpu.VMEM((slot_rows, width), BF),
            pltpu.VMEM((slot_rows, width), BF),
            pltpu.VMEM(dec.shape, BF),
            pltpu.VMEM(dec.shape, BF),
            pltpu.VMEM(dec.shape, BF),
            pltpu.VMEM(dec.shape, BF),
            pltpu.VMEM((width, dec.shape[0]), BF),
            pltpu.VMEM((slot_rows, 128), F32),
            pltpu.SMEM((n,), jnp.int32),
            pltpu.SMEM((questions * slots_per,), jnp.int32),
            pltpu.SemaphoreType.DMA((questions * slots_per,)),
        ],
        compiler_params=pltpu.CompilerParams(vmem_limit_bytes=56 * 2**20),
        name="attend",
    )(ids, infos, dec, cot, table, *weights)


def body(
    decoder_states, cotangent, encoded, valid_len, retrieved, w_query, w_key, w_value, w_output
):
    n = lax.axis_size("enc")
    me = lax.axis_index("enc")
    questions_here, dec_len, width = decoder_states.shape
    passages_here, passage_len, _ = encoded.shape
    per_question = retrieved.shape[1]
    slot_count = questions_here * per_question
    cap = max(2, 2 * slot_count // n)
    table, infos = gather_all(
        encoded.reshape(passages_here * passage_len, width),
        retrieved,
        valid_len.reshape(1, passages_here),
        n,
    )
    all_ids = infos[:, :questions_here, :per_question].reshape(n, slot_count)
    attended, d_decoder, slots, grads = attend_all(
        retrieved,
        infos,
        decoder_states.reshape(questions_here * dec_len, width),
        cotangent.reshape(questions_here * dec_len, width),
        table.reshape(n * passages_here, passage_len, width),
        (w_query, w_key, w_value, w_output),
        n,
        cap,
        (questions_here, dec_len, per_question, passage_len),
    )
    got, summed = return_all(slots.reshape(n, cap * passage_len, width), grads, n)

    ask_owner = all_ids // passages_here
    order = jnp.arange(slot_count, dtype=jnp.int32)
    before = (order[:, None] < order[None, :]).astype(F32)
    mine = ask_owner == me
    ranks = jnp.dot(mine.astype(F32), before)
    hit = mine[:, None, :] & (ranks[:, None, :] == jnp.arange(cap, dtype=F32)[None, :, None])
    local = all_ids - me * passages_here + 1
    wanted = jnp.sum(jnp.where(hit, local[:, None, :], 0), axis=2) - 1
    token_pos = jnp.arange(passage_len, dtype=jnp.int32)
    sent_row = (wanted[:, :, None] * passage_len + token_pos).reshape(n * cap * passage_len)
    sent_row = jnp.where(sent_row < 0, -1, sent_row)
    own_row = jnp.arange(passages_here * passage_len, dtype=jnp.int32)
    select = (own_row[:, None] == sent_row[None, :]).astype(BF)
    d_encoded = jnp.dot(
        select, got.reshape(n * cap * passage_len, width), preferred_element_type=F32
    ).astype(BF)
    return (
        attended.reshape(decoder_states.shape),
        d_decoder.reshape(decoder_states.shape),
        d_encoded.reshape(encoded.shape),
        summed[0],
        summed[1],
        summed[2],
        summed[3],
    )


def solution(mesh):
    both = ("groups", "enc")
    in_specs = (
        P(both, None, None),
        P(both, None, None),
        P(both, None, None),
        P(both),
        P(both, None),
        P(),
        P(),
        P(),
        P(),
    )
    out_specs = (
        P(both, None, None),
        P(both, None, None),
        P(both, None, None),
        P(both, None),
        P(both, None),
        P(both, None),
        P(both, None),
    )
    return jax.shard_map(body, mesh=mesh, in_specs=in_specs, out_specs=out_specs, check_vma=False)
```
